32 devices in a mesh: row: 4 (over x, core), col: 8 (over z, y).
Axes of the slice: x: 2, y: 2, z: 4, core: 2. Of those that a mesh axis runs over, the one named last changes fastest.
Arguments:
- inputs: bfloat16 [512, 8192], P('col', 'row'), may hold values from -6 to 6
- target: bfloat16 [512, 8192], P(None, 'row'), may hold values from -6 to 6
- gate_weight: bfloat16 [8192, 16384], P('row', 'col'), may hold values from -0.0625 to 0.0625
- up_weight: bfloat16 [8192, 16384], P('row', 'col'), may hold values from -0.0625 to 0.0625
- down_weight: bfloat16 [16384, 8192], P('col', 'row'), may hold values from -0.046875 to 0.046875
Outputs:
- output: bfloat16 [512, 8192], P('col', 'row')
- grad_inputs: bfloat16 [512, 8192], P('col', 'row')
- grad_gate_weight: bfloat16 [8192, 16384], P('row', 'col')
- grad_up_weight: bfloat16 [8192, 16384], P('row', 'col')
- grad_down_weight: bfloat16 [16384, 8192], P('col', 'row')
The draws below stay inside these ranges and needn't reach their ends.
All inputs are finite; a program needn't handle non-finite values.
Results may differ from the reference program's by a relative error of at most 0.0065.
Values may be sent and summed in bfloat16 or wider, within the bound.
A program may use at most 128 MiB of HBM per device.

```python
import jax
import jax.numpy as jnp

D = 8192
FF = 16384
TOKENS = 512


def block_levels(own_key, dims, split, least, high):
    factor_of = 1.0
    for axis_at, shards_of in split:
        draws = jax.random.uniform(jax.random.fold_in(jax.random.fold_in(own_key, 6), axis_at), (shards_of,), jnp.float32, least / len(split), high / len(split))
        factor_of = factor_of * jnp.repeat(jnp.exp(draws), dims[axis_at] // shards_of).reshape((-1,) + (1,) * (len(dims) - 1 - axis_at))
    return factor_of


def normal_values(stream_key, extent, scale, most, cuts=(), kind=jnp.bfloat16):
    values = jax.random.normal(stream_key, extent, jnp.float32) * scale
    if len(cuts) > 0:
        values = block_levels(stream_key, extent, cuts, -0.22, 0.18) * values
    return jnp.clip(values, min=-most, max=most).astype(kind)


def setup_inputs(seed: int = 0) -> dict:
    key_of = jax.random.split(jax.random.key(seed), 6)
    return {
        "inputs": normal_values(key_of[0], (TOKENS, D), 1.0, 6.0, ((0, 8), (1, 4))),
        "target": normal_values(key_of[1], (TOKENS, D), 1.0, 6.0, ((1, 4),)),
        "gate_weight": normal_values(key_of[2], (D, FF), D ** -0.5, 0.0625, ((0, 4), (1, 8))),
        "up_weight": normal_values(key_of[3], (D, FF), D ** -0.5, 0.0625, ((0, 4), (1, 8))),
        "down_weight": normal_values(key_of[4], (FF, D), FF ** -0.5, 0.046875, ((0, 8), (1, 4))),
    }


def reference(inputs, target, gate_weight, up_weight, down_weight):
    gate_act = jnp.dot(inputs, gate_weight, preferred_element_type=jnp.float32)
    up_act = jnp.dot(inputs, up_weight, preferred_element_type=jnp.float32)
    sigma = jax.nn.sigmoid(gate_act)
    silu_val = gate_act * sigma
    hidden = (silu_val * up_act).astype(jnp.bfloat16)
    result = jnp.dot(hidden, down_weight, preferred_element_type=jnp.float32)
    output = result.astype(jnp.bfloat16)
    error = (result - target.astype(jnp.float32)).astype(jnp.bfloat16)
    grad_down_weight = jnp.dot(hidden.T, error, preferred_element_type=jnp.float32).astype(jnp.bfloat16)
    grad_hidden = jnp.dot(error, down_weight.T, preferred_element_type=jnp.float32)
    grad_gate = (grad_hidden * up_act * sigma * (1.0 + gate_act * (1.0 - sigma))).astype(jnp.bfloat16)
    grad_up = (grad_hidden * silu_val).astype(jnp.bfloat16)
    grad_gate_weight = jnp.dot(inputs.T, grad_gate, preferred_element_type=jnp.float32).astype(jnp.bfloat16)
    grad_up_weight = jnp.dot(inputs.T, grad_up, preferred_element_type=jnp.float32).astype(jnp.bfloat16)
    grad_inputs = (jnp.dot(grad_gate, gate_weight.T, preferred_element_type=jnp.float32)
                   + jnp.dot(grad_up, up_weight.T, preferred_element_type=jnp.float32)).astype(jnp.bfloat16)
    return output, grad_inputs, grad_gate_weight, grad_up_weight, grad_down_weight
```

```python
import functools

import jax
import jax.numpy as jnp
from jax import lax
from jax.experimental import pallas as pl
from jax.experimental.pallas import tpu as pltpu
from jax.sharding import PartitionSpec as P

BF = jnp.bfloat16
F32 = jnp.float32
CHUNKS = 4
LAG = 4
MESH = pl.DeviceIdType.MESH


class Group:
    def __init__(self, axis, size, other):
        self.axis = axis
        self.line_size = size // 2
        me = lax.axis_index(axis)
        self.pair = lax.rem(me, 2)
        self.line = lax.div(me, 2)
        self.other = lax.axis_index(other)

    def device(self, line, pair):
        at = line * 2 + pair
        return (at, self.other) if self.axis == "row" else (self.other, at)

    def mate(self):
        return self.device(self.line, 1 - self.pair)

    def ahead(self, d):
        return lax.rem(self.line + d, self.line_size)


class Comm:
    def __init__(self, group, send, recv, sent):
        self.g, self.send, self.recv, self.sent = group, send, recv, sent

    def start(self, k, slot, src, dst, dst_slot, device):
        copy = pltpu.make_async_remote_copy(
            src_ref=src,
            dst_ref=dst,
            send_sem=self.send.at[k, slot],
            recv_sem=self.recv.at[k, dst_slot],
            device_id=device,
            device_id_type=MESH,
        )
        copy.start()
        self.sent.append(copy)

    def arrived(self, k, slot, ref):
        pltpu.make_async_remote_copy(
            src_ref=ref,
            dst_ref=ref,
            send_sem=self.send.at[k, slot],
            recv_sem=self.recv.at[k, slot],
            device_id=self.g.mate(),
            device_id_type=MESH,
        ).wait_recv()


class Gather(Comm):
    def spread(self, buf, k, src=None):
        g = self.g
        own = buf.at[k, g.pair, g.line]
        for d in range(1, g.line_size):
            self.start(k, d - 1, own if src is None else src, own, g.line_size - 1 - d, g.device(g.ahead(d), g.pair))

    def forward(self, buf, k):
        g = self.g
        for e in range(g.line_size - 1):
            self.arrived(k, e, buf.at[k, g.pair, g.ahead(1 + e)])
        half = buf.at[k, g.pair]
        self.start(k, g.line_size - 1, half, half, g.line_size - 1, g.mate())

    def finish(self, buf, k):
        self.arrived(k, self.g.line_size - 1, buf.at[k, 1 - self.g.pair])


class Scatter(Comm):
    def exchange(self, part, from_mate, k):
        g = self.g
        self.start(k, g.line_size - 1, part.at[k, 1 - g.pair], from_mate.at[k], g.line_size - 1, g.mate())

    def pass_on(self, part, from_mate, from_line, k):
        g = self.g
        self.arrived(k, g.line_size - 1, from_mate.at[k])
        for d in range(1, g.line_size):
            to = g.ahead(d)
            mine = part.at[k, g.pair, to]
            mine[...] = (mine[...].astype(F32) + from_mate[k, to].astype(F32)).astype(BF)
            slot = g.line_size - 1 - d
            self.start(k, d - 1, mine, from_line.at[k, slot], slot, g.device(to, g.pair))

    def landed(self, from_line, k):
        for e in range(self.g.line_size - 1):
            self.arrived(k, e, from_line.at[k, e])

    def total(self, part, from_mate, from_line, k, cols=slice(None)):
        g = self.g
        acc = part[k, g.pair, g.line, :, cols].astype(F32) + from_mate[k, g.line, :, cols].astype(F32)
        for e in range(g.line_size - 1):
            acc = acc + from_line[k, e, :, cols].astype(F32)
        return acc


def flat(value):
    return value.reshape(-1, value.shape[-1])


def tile_of(size):
    return 256 if size % 256 == 0 else 128


def last_last(left, right):
    return lax.dot_general(left, right, (((1,), (1,)), ((), ())), preferred_element_type=F32)


def layer_kernel(
    rows_n, cols_n,
    x_ref, target_hbm, wg_hbm, wu_hbm, wd_hbm,
    out_ref, gx_ref, tok_hbm, hid_hbm, err_hbm, grad_hbm,
    wg, wu, wd, target, tok, hid, err, grad,
    p1, m1, l1, p2, m2, l2, p3, m3, l3, p4, m4, l4,
    row_send, row_recv, col_send, col_recv, load_sem, store_sem,
):
    hidden = wg.shape[1]
    feats = wg.shape[0]
    chunks = tok.shape[0]
    tb = tok.shape[3]
    row = Group("row", rows_n, "col")
    col = Group("col", cols_n, "row")

    loads = [
        pltpu.make_async_copy(wg_hbm, wg, load_sem.at[0]),
        pltpu.make_async_copy(wu_hbm, wu, load_sem.at[1]),
        pltpu.make_async_copy(wd_hbm, wd, load_sem.at[2]),
        pltpu.make_async_copy(
            target_hbm.at[pl.ds(pl.multiple_of(lax.axis_index("col") * tb * chunks, tb * chunks), tb * chunks)],
            target, load_sem.at[3],
        ),
    ]

    barrier = pltpu.get_barrier_semaphore()
    peers = []
    for g in (row, col):
        peers.append(g.mate())
        for d in range(1, g.line_size):
            peers.append(g.device(g.ahead(d), g.pair))
    for peer in peers:
        pl.semaphore_signal(barrier, inc=1, device_id=peer, device_id_type=MESH)
    pl.semaphore_wait(barrier, len(peers))

    sent, stores = [], []
    ag_in = Gather(col, col_send.at[0], col_recv.at[0], sent)
    rs_act = Scatter(row, row_send.at[0], row_recv.at[0], sent)
    ag_hid = Gather(row, row_send.at[1], row_recv.at[1], sent)
    rs_out = Scatter(col, col_send.at[1], col_recv.at[1], sent)
    ag_err = Gather(col, col_send.at[2], col_recv.at[2], sent)
    rs_hid = Scatter(row, row_send.at[2], row_recv.at[2], sent)
    ag_grad = Gather(row, row_send.at[3], row_recv.at[3], sent)
    rs_in = Scatter(col, col_send.at[3], col_recv.at[3], sent)

    def store(buf, out, i, k):
        copy = pltpu.make_async_copy(buf.at[k], out.at[k], store_sem.at[i, k])
        copy.start()
        stores.append(copy)

    waited = set()

    def need(i):
        if i not in waited:
            waited.add(i)
            loads[i].wait()

    def tiles(size, body):
        t = tile_of(size)

        def step(j, _):
            body(pl.ds(pl.multiple_of(j * t, t), t), j * t)
            return 0

        lax.fori_loop(0, size // t, step, 0)

    def put(part, k, cols, value):
        shape = part.shape[1:4] + (value.shape[-1],)
        part[k, :, :, :, cols] = value.astype(BF).reshape(shape)

    def token_rows(k):
        return pl.ds(k * tb, tb)

    def s_in(k):
        tok[k, col.pair, col.line] = x_ref[token_rows(k), :]
        ag_in.spread(tok, k, x_ref.at[token_rows(k)])

    def s_in_fwd(k):
        ag_in.forward(tok, k)

    def s_act(k):
        ag_in.finish(tok, k)
        need(0)
        need(1)

        def body(cols, at):
            t = cols.size
            put(p1, k, cols, jnp.dot(flat(tok[k]), wg[:, cols], preferred_element_type=F32))
            ups = pl.ds(pl.multiple_of(hidden + at, t), t)
            put(p1, k, ups, jnp.dot(flat(tok[k]), wu[:, cols], preferred_element_type=F32))

        tiles(hidden, body)
        rs_act.exchange(p1, m1, k)
        store(tok, tok_hbm, 0, k)

    def s_act_pass(k):
        rs_act.pass_on(p1, m1, l1, k)

    def s_hid(k):
        rs_act.landed(l1, k)
        gate = rs_act.total(p1, m1, l1, k, pl.ds(0, hidden))
        up = rs_act.total(p1, m1, l1, k, pl.ds(hidden, hidden))
        hid[k, row.pair, row.line] = (gate * jax.nn.sigmoid(gate) * up).astype(BF)
        ag_hid.spread(hid, k)

    def s_hid_fwd(k):
        ag_hid.forward(hid, k)

    def s_out(k):
        ag_hid.finish(hid, k)
        need(2)
        tiles(feats, lambda cols, at: put(
            p2, k, cols, jnp.dot(flat(hid[k]), wd[:, cols], preferred_element_type=F32)))
        rs_out.exchange(p2, m2, k)
        store(hid, hid_hbm, 1, k)

    def s_out_pass(k):
        rs_out.pass_on(p2, m2, l2, k)

    def s_err(k):
        rs_out.landed(l2, k)
        need(3)
        result = rs_out.total(p2, m2, l2, k)
        out_ref[token_rows(k), :] = result.astype(BF)
        err[k, col.pair, col.line] = (result - target[token_rows(k), :].astype(F32)).astype(BF)
        ag_err.spread(err, k)

    def s_err_fwd(k):
        ag_err.forward(err, k)

    def s_ghid(k):
        ag_err.finish(err, k)
        tiles(hidden, lambda cols, at: put(p3, k, cols, last_last(flat(err[k]), wd[cols, :])))
        rs_hid.exchange(p3, m3, k)
        store(err, err_hbm, 2, k)

    def s_ghid_pass(k):
        rs_hid.pass_on(p3, m3, l3, k)

    def s_grads(k):
        rs_hid.landed(l3, k)
        gate = rs_act.total(p1, m1, l1, k, pl.ds(0, hidden))
        up = rs_act.total(p1, m1, l1, k, pl.ds(hidden, hidden))
        dh = rs_hid.total(p3, m3, l3, k)
        sigma = jax.nn.sigmoid(gate)
        grad[k, row.pair, row.line, :, pl.ds(0, hidden)] = (
            dh * up * sigma * (1.0 + gate * (1.0 - sigma))).astype(BF)
        grad[k, row.pair, row.line, :, pl.ds(hidden, hidden)] = (dh * (gate * sigma)).astype(BF)
        ag_grad.spread(grad, k)

    def s_grads_fwd(k):
        ag_grad.forward(grad, k)

    def s_gin(k):
        ag_grad.finish(grad, k)
        tiles(feats, lambda cols, at: put(
            p4, k, cols,
            last_last(flat(grad[k, :, :, :, pl.ds(0, hidden)]), wg[cols, :])
            + last_last(flat(grad[k, :, :, :, pl.ds(hidden, hidden)]), wu[cols, :])))
        rs_in.exchange(p4, m4, k)
        store(grad, grad_hbm, 3, k)

    def s_gin_pass(k):
        rs_in.pass_on(p4, m4, l4, k)

    def s_gout(k):
        rs_in.landed(l4, k)
        gx_ref[token_rows(k), :] = rs_in.total(p4, m4, l4, k).astype(BF)

    stages = [
        s_in_fwd, s_act, s_act_pass, s_hid, s_hid_fwd, s_out, s_out_pass, s_err, s_err_fwd,
        s_ghid, s_ghid_pass, s_grads, s_grads_fwd, s_gin, s_gin_pass, s_gout,
    ]
    for k in range(chunks):
        s_in(k)
    for copy in loads:
        copy.start()
    order = sorted((s + LAG * k, -s, k, s) for k in range(chunks) for s in range(len(stages)))
    for _, _, k, s in order:
        stages[s](k)
    for copy in sent:
        copy.wait_send()
    for copy in stores:
        copy.wait()


def run_layer(rows_n, cols_n, inputs, target, gate_weight, up_weight, down_weight):
    own, feats = inputs.shape
    hidden = gate_weight.shape[1]
    chunks = CHUNKS
    while chunks > 1 and (own % (16 * chunks) or (own * cols_n) % (16 * chunks * rows_n)):
        chunks //= 2
    tb = own // chunks
    rb = own * cols_n // chunks // rows_n
    rl, cl = rows_n // 2, cols_n // 2

    def by_col(width):
        return (chunks, 2, cl, tb, width)

    def by_row(width):
        return (chunks, 2, rl, rb, width)

    def scatter_bufs(line, rows, width):
        return [
            pltpu.VMEM((chunks, 2, line, rows, width), BF),
            pltpu.VMEM((chunks, line, rows, width), BF),
            pltpu.VMEM((chunks, line - 1, rows, width), BF),
        ]

    anywhere = pl.BlockSpec(memory_space=pl.ANY)
    vmem = pl.BlockSpec(memory_space=pltpu.VMEM)
    kept = [by_col(feats), by_row(hidden), by_col(feats), by_row(2 * hidden)]
    return pl.pallas_call(
        functools.partial(layer_kernel, rows_n, cols_n),
        out_shape=[jax.ShapeDtypeStruct((own, feats), BF)] * 2 + [jax.ShapeDtypeStruct(s, BF) for s in kept],
        in_specs=[vmem] + [anywhere] * 4,
        out_specs=[vmem] * 2 + [anywhere] * 4,
        scratch_shapes=[
            pltpu.VMEM(gate_weight.shape, BF),
            pltpu.VMEM(up_weight.shape, BF),
            pltpu.VMEM(down_weight.shape, BF),
            pltpu.VMEM((own, feats), BF),
            *[pltpu.VMEM(s, BF) for s in kept],
            *scatter_bufs(rl, rb, 2 * hidden),
            *scatter_bufs(cl, tb, feats),
            *scatter_bufs(rl, rb, hidden),
            *scatter_bufs(cl, tb, feats),
            pltpu.SemaphoreType.DMA((4, chunks, rl)),
            pltpu.SemaphoreType.DMA((4, chunks, rl)),
            pltpu.SemaphoreType.DMA((4, chunks, cl)),
            pltpu.SemaphoreType.DMA((4, chunks, cl)),
            pltpu.SemaphoreType.DMA((4,)),
            pltpu.SemaphoreType.DMA((4, chunks)),
        ],
        compiler_params=pltpu.CompilerParams(
            collective_id=0, has_side_effects=True, vmem_limit_bytes=60 * 2**20
        ),
        cost_estimate=pl.CostEstimate(
            flops=12 * own * cols_n * feats * hidden,
            bytes_accessed=6 * feats * hidden,
            transcendentals=0,
        ),
        name="layer",
    )(inputs, target, gate_weight, up_weight, down_weight)


def outer_kernel(n, left_ref, *refs):
    turned = left_ref[...].T
    for right_ref, out_ref in zip(refs[:n], refs[n:]):
        out_ref[...] = jnp.dot(turned, right_ref[...], preferred_element_type=F32).astype(BF)


def outer_products(left, rights):
    tokens, wide = left.shape
    step = 256 if wide % 256 == 0 else 128
    width = rights[0][2]
    return pl.pallas_call(
        functools.partial(outer_kernel, len(rights)),
        grid=(wide // step,),
        out_shape=[jax.ShapeDtypeStruct((wide, width), BF)] * len(rights),
        in_specs=[pl.BlockSpec((tokens, step), lambda i: (0, i))]
        + [pl.BlockSpec((tokens, width), functools.partial(lambda at, i: (0, at), at)) for _, at, _ in rights],
        out_specs=[pl.BlockSpec((step, width), lambda i: (i, 0))] * len(rights),
        compiler_params=pltpu.CompilerParams(vmem_limit_bytes=48 * 2**20),
        name="outer",
    )(left, *[r for r, _, _ in rights])


def body(rows_n, cols_n, inputs, target, gate_weight, up_weight, down_weight):
    output, grad_inputs, tok, hid, err, grad = run_layer(
        rows_n, cols_n, inputs, target, gate_weight, up_weight, down_weight)
    tok, hid, err, grad = (flat(a) for a in (tok, hid, err, grad))
    hidden = gate_weight.shape[1]
    grad_gate_weight, grad_up_weight = outer_products(tok, [(grad, 0, hidden), (grad, 1, hidden)])
    (grad_down_weight,) = outer_products(hid, [(err, 0, err.shape[1])])
    return (output, grad_inputs, grad_gate_weight, grad_up_weight, grad_down_weight)


def solution(mesh):
    placed = (P("col", "row"), P(None, "row"), P("row", "col"), P("row", "col"), P("col", "row"))
    return jax.shard_map(
        functools.partial(body, mesh.shape["row"], mesh.shape["col"]),
        mesh=mesh,
        in_specs=placed,
        out_specs=(
            P("col", "row"),
            P("col", "row"),
            P("row", "col"),
            P("row", "col"),
            P("col", "row"),
        ),
        check_vma=False,
    )
```

```python
import functools

import jax
import jax.numpy as jnp
from jax import lax
from jax.experimental import pallas as pl
from jax.experimental.pallas import tpu as pltpu
from jax.sharding import PartitionSpec as P

BF = jnp.bfloat16
F32 = jnp.float32
CHUNKS = 4
TURNS = ("0101023102103102", "1302132023132031", "2030121031230231", "0231202313210323")
MESH = pl.DeviceIdType.MESH


class Group:
    def __init__(self, axis, size, other):
        self.axis = axis
        self.line_size = size // 2
        me = lax.axis_index(axis)
        self.pair = lax.rem(me, 2)
        self.line = lax.div(me, 2)
        self.other = lax.axis_index(other)

    def device(self, line, pair):
        at = line * 2 + pair
        return (at, self.other) if self.axis == "row" else (self.other, at)

    def mate(self):
        return self.device(self.line, 1 - self.pair)

    def ahead(self, d):
        return lax.rem(self.line + d, self.line_size)


class Comm:
    def __init__(self, group, send, recv, sent):
        self.g, self.send, self.recv, self.sent = group, send, recv, sent

    def start(self, k, slot, src, dst, dst_slot, device):
        copy = pltpu.make_async_remote_copy(
            src_ref=src,
            dst_ref=dst,
            send_sem=self.send.at[k, slot],
            recv_sem=self.recv.at[k, dst_slot],
            device_id=device,
            device_id_type=MESH,
        )
        copy.start()
        self.sent.append(copy)

    def arrived(self, k, slot, ref):
        pltpu.make_async_remote_copy(
            src_ref=ref,
            dst_ref=ref,
            send_sem=self.send.at[k, slot],
            recv_sem=self.recv.at[k, slot],
            device_id=self.g.mate(),
            device_id_type=MESH,
        ).wait_recv()


class Gather(Comm):
    def to_mate(self, buf, k, d, src=None):
        g = self.g
        block = buf.at[k, g.pair, g.ahead(d)]
        slot = g.line_size - 1 + d
        self.start(k, slot, block if src is None else src, block, slot, g.mate())

    def spread(self, buf, k, src=None):
        g = self.g
        own = buf.at[k, g.pair, g.line]
        for d in range(1, g.line_size):
            self.start(k, d - 1, own if src is None else src, own, g.line_size - 1 - d, g.device(g.ahead(d), g.pair))
        self.to_mate(buf, k, 0, src)

    def forward(self, buf, k):
        g = self.g
        for d in range(1, g.line_size):
            self.arrived(k, d - 1, buf.at[k, g.pair, g.ahead(d)])
            self.to_mate(buf, k, d)

    def finish(self, buf, k):
        g = self.g
        for d in range(g.line_size):
            self.arrived(k, g.line_size - 1 + d, buf.at[k, 1 - g.pair, g.ahead(d)])


class Scatter(Comm):
    def exchange(self, part, from_mate, k):
        g = self.g
        for d in [*range(1, g.line_size), 0]:
            to = g.ahead(d)
            slot = g.line_size - 1 + d
            self.start(k, slot, part.at[k, 1 - g.pair, to], from_mate.at[k, to], slot, g.mate())

    def pass_on(self, part, from_mate, from_line, k):
        g = self.g
        for d in range(1, g.line_size):
            to = g.ahead(d)
            self.arrived(k, g.line_size - 1 + d, from_mate.at[k, to])
            mine = part.at[k, g.pair, to]
            mine[...] = (mine[...].astype(F32) + from_mate[k, to].astype(F32)).astype(BF)
            slot = g.line_size - 1 - d
            self.start(k, d - 1, mine, from_line.at[k, slot], slot, g.device(to, g.pair))

    def landed(self, from_mate, from_line, k):
        g = self.g
        self.arrived(k, g.line_size - 1, from_mate.at[k, g.line])
        for e in range(g.line_size - 1):
            self.arrived(k, e, from_line.at[k, e])

    def total(self, part, from_mate, from_line, k, cols=slice(None)):
        g = self.g
        acc = part[k, g.pair, g.line, :, cols].astype(F32) + from_mate[k, g.line, :, cols].astype(F32)
        for e in range(g.line_size - 1):
            acc = acc + from_line[k, e, :, cols].astype(F32)
        return acc


def flat(value):
    return value.reshape(-1, value.shape[-1])


def turns(chunks, stages):
    if chunks == 4 and stages == 16:
        line = [int(c) for c in "".join(TURNS)]
    else:
        line = [k for _, _, k in sorted((s + k, -s, k) for k in range(chunks) for s in range(stages))]
    done = [0] * chunks
    order = []
    for k in line:
        order.append((k, done[k]))
        done[k] += 1
    return order


def tile_of(size):
    return 256 if size % 256 == 0 else 128


def last_last(left, right):
    return lax.dot_general(left, right, (((1,), (1,)), ((), ())), preferred_element_type=F32)


def layer_kernel(
    rows_n, cols_n,
    x_ref, target_hbm, wg_hbm, wu_hbm, wd_hbm,
    out_ref, gx_ref, tok_hbm, hid_hbm, err_hbm, grad_hbm,
    wg, wu, wd, target, tok, hid, err, grad,
    p1, m1, l1, p2, m2, l2, p3, m3, l3, p4, m4, l4,
    row_send, row_recv, col_send, col_recv, load_sem, store_sem,
):
    hidden = wg.shape[1]
    feats = wg.shape[0]
    chunks = tok.shape[0]
    tb = tok.shape[3]
    row = Group("row", rows_n, "col")
    col = Group("col", cols_n, "row")

    loads = [
        pltpu.make_async_copy(wg_hbm, wg, load_sem.at[0]),
        pltpu.make_async_copy(wu_hbm, wu, load_sem.at[1]),
        pltpu.make_async_copy(wd_hbm, wd, load_sem.at[2]),
        pltpu.make_async_copy(
            target_hbm.at[pl.ds(pl.multiple_of(lax.axis_index("col") * tb * chunks, tb * chunks), tb * chunks)],
            target, load_sem.at[3],
        ),
    ]

    barrier = pltpu.get_barrier_semaphore()
    peers = []
    for g in (row, col):
        peers.append(g.mate())
        for d in range(1, g.line_size):
            peers.append(g.device(g.ahead(d), g.pair))
    for peer in peers:
        pl.semaphore_signal(barrier, inc=1, device_id=peer, device_id_type=MESH)
    pl.semaphore_wait(barrier, len(peers))

    sent, stores = [], []
    ag_in = Gather(col, col_send.at[0], col_recv.at[0], sent)
    rs_act = Scatter(row, row_send.at[0], row_recv.at[0], sent)
    ag_hid = Gather(row, row_send.at[1], row_recv.at[1], sent)
    rs_out = Scatter(col, col_send.at[1], col_recv.at[1], sent)
    ag_err = Gather(col, col_send.at[2], col_recv.at[2], sent)
    rs_hid = Scatter(row, row_send.at[2], row_recv.at[2], sent)
    ag_grad = Gather(row, row_send.at[3], row_recv.at[3], sent)
    rs_in = Scatter(col, col_send.at[3], col_recv.at[3], sent)

    def store(buf, out, i, k):
        copy = pltpu.make_async_copy(buf.at[k], out.at[k], store_sem.at[i, k])
        copy.start()
        stores.append(copy)

    waited = set()

    def need(i):
        if i not in waited:
            waited.add(i)
            loads[i].wait()

    def tiles(size, body):
        t = tile_of(size)

        def step(j, _):
            body(pl.ds(pl.multiple_of(j * t, t), t), j * t)
            return 0

        lax.fori_loop(0, size // t, step, 0)

    def put(part, k, cols, value):
        shape = part.shape[1:4] + (value.shape[-1],)
        part[k, :, :, :, cols] = value.astype(BF).reshape(shape)

    def token_rows(k):
        return pl.ds(k * tb, tb)

    def s_in(k):
        tok[k, col.pair, col.line] = x_ref[token_rows(k), :]
        ag_in.spread(tok, k, x_ref.at[token_rows(k)])

    def s_in_fwd(k):
        ag_in.forward(tok, k)

    def s_act(k):
        ag_in.finish(tok, k)
        need(0)
        need(1)

        def body(cols, at):
            t = cols.size
            put(p1, k, cols, jnp.dot(flat(tok[k]), wg[:, cols], preferred_element_type=F32))
            ups = pl.ds(pl.multiple_of(hidden + at, t), t)
            put(p1, k, ups, jnp.dot(flat(tok[k]), wu[:, cols], preferred_element_type=F32))

        tiles(hidden, body)
        rs_act.exchange(p1, m1, k)
        store(tok, tok_hbm, 0, k)

    def s_act_pass(k):
        rs_act.pass_on(p1, m1, l1, k)

    def s_hid(k):
        rs_act.landed(m1, l1, k)
        gate = rs_act.total(p1, m1, l1, k, pl.ds(0, hidden))
        up = rs_act.total(p1, m1, l1, k, pl.ds(hidden, hidden))
        hid[k, row.pair, row.line] = (gate * jax.nn.sigmoid(gate) * up).astype(BF)
        ag_hid.spread(hid, k)

    def s_hid_fwd(k):
        ag_hid.forward(hid, k)

    def s_out(k):
        ag_hid.finish(hid, k)
        need(2)
        tiles(feats, lambda cols, at: put(
            p2, k, cols, jnp.dot(flat(hid[k]), wd[:, cols], preferred_element_type=F32)))
        rs_out.exchange(p2, m2, k)
        store(hid, hid_hbm, 1, k)

    def s_out_pass(k):
        rs_out.pass_on(p2, m2, l2, k)

    def s_err(k):
        rs_out.landed(m2, l2, k)
        need(3)
        result = rs_out.total(p2, m2, l2, k)
        out_ref[token_rows(k), :] = result.astype(BF)
        err[k, col.pair, col.line] = (result - target[token_rows(k), :].astype(F32)).astype(BF)
        ag_err.spread(err, k)

    def s_err_fwd(k):
        ag_err.forward(err, k)

    def s_ghid(k):
        ag_err.finish(err, k)
        tiles(hidden, lambda cols, at: put(p3, k, cols, last_last(flat(err[k]), wd[cols, :])))
        rs_hid.exchange(p3, m3, k)
        store(err, err_hbm, 2, k)

    def s_ghid_pass(k):
        rs_hid.pass_on(p3, m3, l3, k)

    def s_grads(k):
        rs_hid.landed(m3, l3, k)
        gate = rs_act.total(p1, m1, l1, k, pl.ds(0, hidden))
        up = rs_act.total(p1, m1, l1, k, pl.ds(hidden, hidden))
        dh = rs_hid.total(p3, m3, l3, k)
        sigma = jax.nn.sigmoid(gate)
        grad[k, row.pair, row.line, :, pl.ds(0, hidden)] = (
            dh * up * sigma * (1.0 + gate * (1.0 - sigma))).astype(BF)
        grad[k, row.pair, row.line, :, pl.ds(hidden, hidden)] = (dh * (gate * sigma)).astype(BF)
        ag_grad.spread(grad, k)

    def s_grads_fwd(k):
        ag_grad.forward(grad, k)

    def s_gin(k):
        ag_grad.finish(grad, k)
        tiles(feats, lambda cols, at: put(
            p4, k, cols,
            last_last(flat(grad[k, :, :, :, pl.ds(0, hidden)]), wg[cols, :])
            + last_last(flat(grad[k, :, :, :, pl.ds(hidden, hidden)]), wu[cols, :])))
        rs_in.exchange(p4, m4, k)
        store(grad, grad_hbm, 3, k)

    def s_gin_pass(k):
        rs_in.pass_on(p4, m4, l4, k)

    def s_gout(k):
        rs_in.landed(m4, l4, k)
        gx_ref[token_rows(k), :] = rs_in.total(p4, m4, l4, k).astype(BF)

    stages = [
        s_in_fwd, s_act, s_act_pass, s_hid, s_hid_fwd, s_out, s_out_pass, s_err, s_err_fwd,
        s_ghid, s_ghid_pass, s_grads, s_grads_fwd, s_gin, s_gin_pass, s_gout,
    ]
    for k in range(chunks):
        s_in(k)
    for copy in loads:
        copy.start()
    for k, s in turns(chunks, len(stages)):
        stages[s](k)
    for copy in sent:
        copy.wait_send()
    for copy in stores:
        copy.wait()


def run_layer(rows_n, cols_n, inputs, target, gate_weight, up_weight, down_weight):
    own, feats = inputs.shape
    hidden = gate_weight.shape[1]
    chunks = CHUNKS
    while chunks > 1 and (own % (16 * chunks) or (own * cols_n) % (16 * chunks * rows_n)):
        chunks //= 2
    tb = own // chunks
    rb = own * cols_n // chunks // rows_n
    rl, cl = rows_n // 2, cols_n // 2

    def by_col(width):
        return (chunks, 2, cl, tb, width)

    def by_row(width):
        return (chunks, 2, rl, rb, width)

    def scatter_bufs(line, rows, width):
        return [
            pltpu.VMEM((chunks, 2, line, rows, width), BF),
            pltpu.VMEM((chunks, line, rows, width), BF),
            pltpu.VMEM((chunks, line - 1, rows, width), BF),
        ]

    anywhere = pl.BlockSpec(memory_space=pl.ANY)
    vmem = pl.BlockSpec(memory_space=pltpu.VMEM)
    kept = [by_col(feats), by_row(hidden), by_col(feats), by_row(2 * hidden)]
    return pl.pallas_call(
        functools.partial(layer_kernel, rows_n, cols_n),
        out_shape=[jax.ShapeDtypeStruct((own, feats), BF)] * 2 + [jax.ShapeDtypeStruct(s, BF) for s in kept],
        in_specs=[vmem] + [anywhere] * 4,
        out_specs=[vmem] * 2 + [anywhere] * 4,
        scratch_shapes=[
            pltpu.VMEM(gate_weight.shape, BF),
            pltpu.VMEM(up_weight.shape, BF),
            pltpu.VMEM(down_weight.shape, BF),
            pltpu.VMEM((own, feats), BF),
            *[pltpu.VMEM(s, BF) for s in kept],
            *scatter_bufs(rl, rb, 2 * hidden),
            *scatter_bufs(cl, tb, feats),
            *scatter_bufs(rl, rb, hidden),
            *scatter_bufs(cl, tb, feats),
            pltpu.SemaphoreType.DMA((4, chunks, 2 * rl - 1)),
            pltpu.SemaphoreType.DMA((4, chunks, 2 * rl - 1)),
            pltpu.SemaphoreType.DMA((4, chunks, 2 * cl - 1)),
            pltpu.SemaphoreType.DMA((4, chunks, 2 * cl - 1)),
            pltpu.SemaphoreType.DMA((4,)),
            pltpu.SemaphoreType.DMA((4, chunks)),
        ],
        compiler_params=pltpu.CompilerParams(
            collective_id=0, has_side_effects=True, vmem_limit_bytes=60 * 2**20
        ),
        cost_estimate=pl.CostEstimate(
            flops=12 * own * cols_n * feats * hidden,
            bytes_accessed=6 * feats * hidden,
            transcendentals=0,
        ),
        name="layer",
    )(inputs, target, gate_weight, up_weight, down_weight)


def outer_kernel(n, left_ref, *refs):
    turned = left_ref[...].T
    for right_ref, out_ref in zip(refs[:n], refs[n:]):
        out_ref[...] = jnp.dot(turned, right_ref[...], preferred_element_type=F32).astype(BF)


def outer_products(left, rights):
    tokens, wide = left.shape
    step = next(t for t in (512, 256, 128) if wide % t == 0)
    width = rights[0][2]
    return pl.pallas_call(
        functools.partial(outer_kernel, len(rights)),
        grid=(wide // step,),
        out_shape=[jax.ShapeDtypeStruct((wide, width), BF)] * len(rights),
        in_specs=[pl.BlockSpec((tokens, step), lambda i: (0, i))]
        + [pl.BlockSpec((tokens, width), functools.partial(lambda at, i: (0, at), at)) for _, at, _ in rights],
        out_specs=[pl.BlockSpec((step, width), lambda i: (i, 0))] * len(rights),
        compiler_params=pltpu.CompilerParams(vmem_limit_bytes=48 * 2**20),
        name="outer",
    )(left, *[r for r, _, _ in rights])


def body(rows_n, cols_n, inputs, target, gate_weight, up_weight, down_weight):
    output, grad_inputs, tok, hid, err, grad = run_layer(
        rows_n, cols_n, inputs, target, gate_weight, up_weight, down_weight)
    tok, hid, err, grad = (flat(a) for a in (tok, hid, err, grad))
    hidden = gate_weight.shape[1]
    grad_gate_weight, grad_up_weight = outer_products(tok, [(grad, 0, hidden), (grad, 1, hidden)])
    (grad_down_weight,) = outer_products(hid, [(err, 0, err.shape[1])])
    return (output, grad_inputs, grad_gate_weight, grad_up_weight, grad_down_weight)


def solution(mesh):
    placed = (P("col", "row"), P(None, "row"), P("row", "col"), P("row", "col"), P("col", "row"))
    return jax.shard_map(
        functools.partial(body, mesh.shape["row"], mesh.shape["col"]),
        mesh=mesh,
        in_specs=placed,
        out_specs=(
            P("col", "row"),
            P("col", "row"),
            P("row", "col"),
            P("row", "col"),
            P("col", "row"),
        ),
        check_vma=False,
    )
```

```python
import functools

import jax
import jax.numpy as jnp
from jax import lax
from jax.experimental import pallas as pl
from jax.experimental.pallas import tpu as pltpu
from jax.sharding import PartitionSpec as P

BF = jnp.bfloat16
F32 = jnp.float32
CHUNKS = 4
TURNS = ("0102012013020130", "1213202130231302", "0130213120213023", "13120321032132")
MESH = pl.DeviceIdType.MESH


class Group:
    def __init__(self, axis, size, other):
        self.axis = axis
        self.line_size = size // 2
        me = lax.axis_index(axis)
        self.pair = lax.rem(me, 2)
        self.line = lax.div(me, 2)
        self.other = lax.axis_index(other)

    def device(self, line, pair):
        at = line * 2 + pair
        return (at, self.other) if self.axis == "row" else (self.other, at)

    def mate(self):
        return self.device(self.line, 1 - self.pair)

    def ahead(self, d):
        return lax.rem(self.line + d, self.line_size)


class Comm:
    def __init__(self, group, send, recv, sent):
        self.g, self.send, self.recv, self.sent = group, send, recv, sent

    def start(self, k, slot, src, dst, dst_slot, device):
        copy = pltpu.make_async_remote_copy(
            src_ref=src,
            dst_ref=dst,
            send_sem=self.send.at[k, slot],
            recv_sem=self.recv.at[k, dst_slot],
            device_id=device,
            device_id_type=MESH,
        )
        copy.start()
        self.sent.append(copy)

    def arrived(self, k, slot, ref):
        pltpu.make_async_remote_copy(
            src_ref=ref,
            dst_ref=ref,
            send_sem=self.send.at[k, slot],
            recv_sem=self.recv.at[k, slot],
            device_id=self.g.mate(),
            device_id_type=MESH,
        ).wait_recv()


class Gather(Comm):
    def to_mate(self, buf, k, d, src=None):
        g = self.g
        block = buf.at[k, g.pair, g.ahead(d)]
        slot = g.line_size - 1 + d
        self.start(k, slot, block if src is None else src, block, slot, g.mate())

    def spread(self, buf, k, src=None):
        g = self.g
        own = buf.at[k, g.pair, g.line]
        for d in range(1, g.line_size):
            self.start(k, d - 1, own if src is None else src, own, g.line_size - 1 - d, g.device(g.ahead(d), g.pair))
        self.to_mate(buf, k, 0, src)

    def forward(self, buf, k):
        g = self.g
        for d in range(1, g.line_size):
            self.arrived(k, d - 1, buf.at[k, g.pair, g.ahead(d)])
            self.to_mate(buf, k, d)

    def finish(self, buf, k):
        g = self.g
        for d in range(g.line_size):
            self.arrived(k, g.line_size - 1 + d, buf.at[k, 1 - g.pair, g.ahead(d)])


class Scatter(Comm):
    def exchange(self, part, from_mate, k):
        g = self.g
        for d in [*range(1, g.line_size), 0]:
            to = g.ahead(d)
            slot = g.line_size - 1 + d
            self.start(k, slot, part.at[k, 1 - g.pair, to], from_mate.at[k, to], slot, g.mate())

    def pass_on(self, part, from_mate, from_line, k):
        g = self.g
        for d in range(1, g.line_size):
            to = g.ahead(d)
            self.arrived(k, g.line_size - 1 + d, from_mate.at[k, to])
            mine = part.at[k, g.pair, to]
            mine[...] = (mine[...].astype(F32) + from_mate[k, to].astype(F32)).astype(BF)
            slot = g.line_size - 1 - d
            self.start(k, d - 1, mine, from_line.at[k, slot], slot, g.device(to, g.pair))

    def landed(self, from_mate, from_line, k):
        g = self.g
        self.arrived(k, g.line_size - 1, from_mate.at[k, g.line])
        for e in range(g.line_size - 1):
            self.arrived(k, e, from_line.at[k, e])

    def total(self, part, from_mate, from_line, k, cols=slice(None)):
        g = self.g
        acc = part[k, g.pair, g.line, :, cols].astype(F32) + from_mate[k, g.line, :, cols].astype(F32)
        for e in range(g.line_size - 1):
            acc = acc + from_line[k, e, :, cols].astype(F32)
        return acc


def flat(value):
    return value.reshape(-1, value.shape[-1])


def turns(chunks, stages):
    if chunks == 4 and stages == 16:
        line = [int(c) for c in "".join(TURNS)]
    else:
        line = [k for _, _, k in sorted((s + k, -s, k) for k in range(chunks) for s in range(stages))]
    for _ in range(line.count(chunks - 1) - (stages - 2)):
        line.pop(len(line) - 1 - line[::-1].index(chunks - 1))
    done = [0] * chunks
    order = []
    for k in line:
        order.append((k, done[k]))
        done[k] += 1
    return order


def tile_of(size):
    return next(t for t in (512, 256, 128) if size % t == 0)


def last_last(left, right):
    return lax.dot_general(left, right, (((1,), (1,)), ((), ())), preferred_element_type=F32)


def layer_kernel(
    rows_n, cols_n,
    x_ref, target_hbm, wg_hbm, wu_hbm, wd_hbm,
    out_ref, gx_ref, tok_hbm, hid_hbm, err_hbm, grad_hbm, part_hbm,
    wg, wu, wd, target, tok, hid, err, grad,
    p1, m1, l1, p2, m2, l2, p3, m3, l3, p4, m4, l4,
    row_send, row_recv, col_send, col_recv, load_sem, store_sem,
):
    hidden = wg.shape[1]
    feats = wg.shape[0]
    chunks = tok.shape[0]
    tb = tok.shape[3]
    row = Group("row", rows_n, "col")
    col = Group("col", cols_n, "row")

    loads = [
        pltpu.make_async_copy(wg_hbm, wg, load_sem.at[0]),
        pltpu.make_async_copy(wu_hbm, wu, load_sem.at[1]),
        pltpu.make_async_copy(wd_hbm, wd, load_sem.at[2]),
        pltpu.make_async_copy(
            target_hbm.at[pl.ds(pl.multiple_of(lax.axis_index("col") * tb * chunks, tb * chunks), tb * chunks)],
            target, load_sem.at[3],
        ),
    ]

    barrier = pltpu.get_barrier_semaphore()
    peers = []
    for g in (row, col):
        peers.append(g.mate())
        for d in range(1, g.line_size):
            peers.append(g.device(g.ahead(d), g.pair))
    for peer in peers:
        pl.semaphore_signal(barrier, inc=1, device_id=peer, device_id_type=MESH)
    pl.semaphore_wait(barrier, len(peers))

    sent, stores = [], []
    ag_in = Gather(col, col_send.at[0], col_recv.at[0], sent)
    rs_act = Scatter(row, row_send.at[0], row_recv.at[0], sent)
    ag_hid = Gather(row, row_send.at[1], row_recv.at[1], sent)
    rs_out = Scatter(col, col_send.at[1], col_recv.at[1], sent)
    ag_err = Gather(col, col_send.at[2], col_recv.at[2], sent)
    rs_hid = Scatter(row, row_send.at[2], row_recv.at[2], sent)
    ag_grad = Gather(row, row_send.at[3], row_recv.at[3], sent)
    rs_in = Scatter(col, col_send.at[3], col_recv.at[3], sent)

    def store(buf, out, i, k):
        copy = pltpu.make_async_copy(buf.at[k], out.at[k], store_sem.at[i, k])
        copy.start()
        stores.append(copy)

    waited = set()

    def need(i):
        if i not in waited:
            waited.add(i)
            loads[i].wait()

    def tiles(size, body):
        t = tile_of(size)

        def step(j, _):
            body(pl.ds(pl.multiple_of(j * t, t), t), j * t)
            return 0

        lax.fori_loop(0, size // t, step, 0)

    def put(part, k, cols, value):
        shape = part.shape[1:4] + (value.shape[-1],)
        part[k, :, :, :, cols] = value.astype(BF).reshape(shape)

    def token_rows(k):
        return pl.ds(k * tb, tb)

    def s_in(k):
        tok[k, col.pair, col.line] = x_ref[token_rows(k), :]
        ag_in.spread(tok, k, x_ref.at[token_rows(k)])

    def s_in_fwd(k):
        ag_in.forward(tok, k)

    def s_act(k):
        ag_in.finish(tok, k)
        need(0)
        need(1)

        def body(cols, at):
            t = cols.size
            put(p1, k, cols, jnp.dot(flat(tok[k]), wg[:, cols], preferred_element_type=F32))
            ups = pl.ds(pl.multiple_of(hidden + at, t), t)
            put(p1, k, ups, jnp.dot(flat(tok[k]), wu[:, cols], preferred_element_type=F32))

        tiles(hidden, body)
        rs_act.exchange(p1, m1, k)
        store(tok, tok_hbm, 0, k)

    def s_act_pass(k):
        rs_act.pass_on(p1, m1, l1, k)

    def s_hid(k):
        rs_act.landed(m1, l1, k)
        gate = rs_act.total(p1, m1, l1, k, pl.ds(0, hidden))
        up = rs_act.total(p1, m1, l1, k, pl.ds(hidden, hidden))
        hid[k, row.pair, row.line] = (gate * jax.nn.sigmoid(gate) * up).astype(BF)
        ag_hid.spread(hid, k)

    def s_hid_fwd(k):
        ag_hid.forward(hid, k)

    def s_out(k):
        ag_hid.finish(hid, k)
        need(2)
        tiles(feats, lambda cols, at: put(
            p2, k, cols, jnp.dot(flat(hid[k]), wd[:, cols], preferred_element_type=F32)))
        rs_out.exchange(p2, m2, k)
        store(hid, hid_hbm, 1, k)

    def s_out_pass(k):
        rs_out.pass_on(p2, m2, l2, k)

    def s_err(k):
        rs_out.landed(m2, l2, k)
        need(3)
        result = rs_out.total(p2, m2, l2, k)
        out_ref[token_rows(k), :] = result.astype(BF)
        err[k, col.pair, col.line] = (result - target[token_rows(k), :].astype(F32)).astype(BF)
        ag_err.spread(err, k)

    def s_err_fwd(k):
        ag_err.forward(err, k)

    def s_ghid(k):
        ag_err.finish(err, k)
        tiles(hidden, lambda cols, at: put(p3, k, cols, last_last(flat(err[k]), wd[cols, :])))
        rs_hid.exchange(p3, m3, k)
        store(err, err_hbm, 2, k)

    def s_ghid_pass(k):
        rs_hid.pass_on(p3, m3, l3, k)

    def s_grads(k):
        rs_hid.landed(m3, l3, k)
        gate = rs_act.total(p1, m1, l1, k, pl.ds(0, hidden))
        up = rs_act.total(p1, m1, l1, k, pl.ds(hidden, hidden))
        dh = rs_hid.total(p3, m3, l3, k)
        sigma = jax.nn.sigmoid(gate)
        grad[k, row.pair, row.line, :, pl.ds(0, hidden)] = (
            dh * up * sigma * (1.0 + gate * (1.0 - sigma))).astype(BF)
        grad[k, row.pair, row.line, :, pl.ds(hidden, hidden)] = (dh * (gate * sigma)).astype(BF)
        ag_grad.spread(grad, k)

    def s_grads_fwd(k):
        ag_grad.forward(grad, k)

    def s_gin(k):
        ag_grad.finish(grad, k)
        tiles(feats, lambda cols, at: put(
            p4, k, cols,
            last_last(flat(grad[k, :, :, :, pl.ds(0, hidden)]), wg[cols, :])
            + last_last(flat(grad[k, :, :, :, pl.ds(hidden, hidden)]), wu[cols, :])))
        store(grad, grad_hbm, 3, k)
        if k < chunks - 1:
            rs_in.exchange(p4, m4, k)
            return
        copy = pltpu.make_async_copy(p4.at[k], part_hbm, load_sem.at[4])
        copy.start()
        stores.append(copy)

    def s_gin_pass(k):
        rs_in.pass_on(p4, m4, l4, k)

    def s_gout(k):
        rs_in.landed(m4, l4, k)
        gx_ref[token_rows(k), :] = rs_in.total(p4, m4, l4, k).astype(BF)

    stages = [
        s_in_fwd, s_act, s_act_pass, s_hid, s_hid_fwd, s_out, s_out_pass, s_err, s_err_fwd,
        s_ghid, s_ghid_pass, s_grads, s_grads_fwd, s_gin, s_gin_pass, s_gout,
    ]
    for k in range(chunks):
        s_in(k)
    for copy in loads:
        copy.start()
    for k, s in turns(chunks, len(stages)):
        stages[s](k)
    for copy in sent:
        copy.wait_send()
    for copy in stores:
        copy.wait()


def run_layer(rows_n, cols_n, inputs, target, gate_weight, up_weight, down_weight):
    own, feats = inputs.shape
    hidden = gate_weight.shape[1]
    chunks = CHUNKS
    while chunks > 1 and (own % (16 * chunks) or (own * cols_n) % (16 * chunks * rows_n)):
        chunks //= 2
    tb = own // chunks
    rb = own * cols_n // chunks // rows_n
    rl, cl = rows_n // 2, cols_n // 2

    def by_col(width):
        return (chunks, 2, cl, tb, width)

    def by_row(width):
        return (chunks, 2, rl, rb, width)

    def scatter_bufs(line, rows, width):
        return [
            pltpu.VMEM((chunks, 2, line, rows, width), BF),
            pltpu.VMEM((chunks, line, rows, width), BF),
            pltpu.VMEM((chunks, line - 1, rows, width), BF),
        ]

    anywhere = pl.BlockSpec(memory_space=pl.ANY)
    vmem = pl.BlockSpec(memory_space=pltpu.VMEM)
    kept = [by_col(feats), by_row(hidden), by_col(feats), by_row(2 * hidden)]
    return pl.pallas_call(
        functools.partial(layer_kernel, rows_n, cols_n),
        out_shape=[
            jax.ShapeDtypeStruct(s, BF)
            for s in [(own, feats), (max(own - tb, tb), feats), *kept, by_col(feats)[1:]]
        ],
        in_specs=[vmem] + [anywhere] * 4,
        out_specs=[vmem] * 2 + [anywhere] * 5,
        scratch_shapes=[
            pltpu.VMEM(gate_weight.shape, BF),
            pltpu.VMEM(up_weight.shape, BF),
            pltpu.VMEM(down_weight.shape, BF),
            pltpu.VMEM((own, feats), BF),
            *[pltpu.VMEM(s, BF) for s in kept],
            *scatter_bufs(rl, rb, 2 * hidden),
            *scatter_bufs(cl, tb, feats),
            *scatter_bufs(rl, rb, hidden),
            *scatter_bufs(cl, tb, feats),
            pltpu.SemaphoreType.DMA((4, chunks, 2 * rl - 1)),
            pltpu.SemaphoreType.DMA((4, chunks, 2 * rl - 1)),
            pltpu.SemaphoreType.DMA((4, chunks, 2 * cl - 1)),
            pltpu.SemaphoreType.DMA((4, chunks, 2 * cl - 1)),
            pltpu.SemaphoreType.DMA((5,)),
            pltpu.SemaphoreType.DMA((4, chunks)),
        ],
        compiler_params=pltpu.CompilerParams(
            collective_id=0, has_side_effects=True, vmem_limit_bytes=60 * 2**20
        ),
        cost_estimate=pl.CostEstimate(
            flops=12 * own * cols_n * feats * hidden,
            bytes_accessed=6 * feats * hidden,
            transcendentals=0,
        ),
        name="layer",
    )(inputs, target, gate_weight, up_weight, down_weight)


def finish_scatter(part, cols_n):
    line_n = cols_n // 2
    me = lax.axis_index("col")
    pair, line = lax.rem(me, 2), lax.div(me, 2)
    theirs = lax.dynamic_index_in_dim(part, 1 - pair, 0, keepdims=False)
    mine = lax.dynamic_index_in_dim(part, pair, 0, keepdims=False).astype(F32)
    got = lax.ppermute(theirs, "col", [(c, c + 1 - 2 * (c % 2)) for c in range(cols_n)])
    mine = mine + got.astype(F32)
    total = lax.dynamic_index_in_dim(mine, line, 0, keepdims=False)
    for d in range(1, line_n):
        block = lax.dynamic_index_in_dim(mine, lax.rem(line + d, line_n), 0, keepdims=False).astype(BF)
        pairs = [(c, ((c // 2 + d) % line_n) * 2 + c % 2) for c in range(cols_n)]
        total = total + lax.ppermute(block, "col", pairs).astype(F32)
    return total.astype(BF)


def outer_kernel(n, left_ref, *refs):
    turned = left_ref[...].T
    for right_ref, out_ref in zip(refs[:n], refs[n:]):
        out_ref[...] = jnp.dot(turned, right_ref[...], preferred_element_type=F32).astype(BF)


def outer_products(left, rights):
    tokens, wide = left.shape
    step = next(t for t in (512, 256, 128) if wide % t == 0)
    width = rights[0][2]
    return pl.pallas_call(
        functools.partial(outer_kernel, len(rights)),
        grid=(wide // step,),
        out_shape=[jax.ShapeDtypeStruct((wide, width), BF)] * len(rights),
        in_specs=[pl.BlockSpec((tokens, step), lambda i: (0, i))]
        + [pl.BlockSpec((tokens, width), functools.partial(lambda at, i: (0, at), at)) for _, at, _ in rights],
        out_specs=[pl.BlockSpec((step, width), lambda i: (i, 0))] * len(rights),
        compiler_params=pltpu.CompilerParams(vmem_limit_bytes=48 * 2**20),
        cost_estimate=pl.CostEstimate(
            flops=2 * tokens * wide * width * len(rights),
            bytes_accessed=2 * (tokens * wide + (tokens + wide) * width * len(rights)),
            transcendentals=0,
        ),
        name="outer",
    )(left, *[r for r, _, _ in rights])


def body(rows_n, cols_n, inputs, target, gate_weight, up_weight, down_weight):
    output, first_rows, tok, hid, err, grad, part = run_layer(
        rows_n, cols_n, inputs, target, gate_weight, up_weight, down_weight)
    last_rows = finish_scatter(part, cols_n)
    kept_rows = inputs.shape[0] - last_rows.shape[0]
    grad_inputs = jnp.concatenate([first_rows[:kept_rows], last_rows], axis=0)
    tok, hid, err, grad = (flat(a) for a in (tok, hid, err, grad))
    hidden = gate_weight.shape[1]
    grad_gate_weight, grad_up_weight = outer_products(tok, [(grad, 0, hidden), (grad, 1, hidden)])
    (grad_down_weight,) = outer_products(hid, [(err, 0, err.shape[1])])
    return (output, grad_inputs, grad_gate_weight, grad_up_weight, grad_down_weight)


def solution(mesh):
    placed = (P("col", "row"), P(None, "row"), P("row", "col"), P("row", "col"), P("col", "row"))
    return jax.shard_map(
        functools.partial(body, mesh.shape["row"], mesh.shape["col"]),
        mesh=mesh,
        in_specs=placed,
        out_specs=(
            P("col", "row"),
            P("col", "row"),
            P("row", "col"),
            P("row", "col"),
            P("col", "row"),
        ),
        check_vma=False,
    )
```

```python
import functools

import jax
import jax.numpy as jnp
from jax import lax
from jax.experimental import pallas as pl
from jax.experimental.pallas import tpu as pltpu
from jax.sharding import PartitionSpec as P

BF = jnp.bfloat16
F32 = jnp.float32
CHUNKS = 4
TURNS = ("0102012013020130", "1213202130231302", "0130213120213023", "13120321032132")
MESH = pl.DeviceIdType.MESH


class Group:
    def __init__(self, axis, size, other):
        self.axis = axis
        self.line_size = size // 2
        me = lax.axis_index(axis)
        self.pair = lax.rem(me, 2)
        self.line = lax.div(me, 2)
        self.other = lax.axis_index(other)

    def device(self, line, pair):
        at = line * 2 + pair
        return (at, self.other) if self.axis == "row" else (self.other, at)

    def mate(self):
        return self.device(self.line, 1 - self.pair)

    def ahead(self, d):
        return lax.rem(self.line + d, self.line_size)


class Comm:
    def __init__(self, group, send, recv, sent):
        self.g, self.send, self.recv, self.sent = group, send, recv, sent

    def start(self, k, slot, src, dst, dst_slot, device):
        copy = pltpu.make_async_remote_copy(
            src_ref=src,
            dst_ref=dst,
            send_sem=self.send.at[k, slot],
            recv_sem=self.recv.at[k, dst_slot],
            device_id=device,
            device_id_type=MESH,
        )
        copy.start()
        self.sent.append(copy)

    def arrived(self, k, slot, ref):
        pltpu.make_async_remote_copy(
            src_ref=ref,
            dst_ref=ref,
            send_sem=self.send.at[k, slot],
            recv_sem=self.recv.at[k, slot],
            device_id=self.g.mate(),
            device_id_type=MESH,
        ).wait_recv()


class Gather(Comm):
    def to_mate(self, buf, k, d, src=None):
        g = self.g
        block = buf.at[k, g.pair, g.ahead(d)]
        slot = g.line_size - 1 + d
        self.start(k, slot, block if src is None else src, block, slot, g.mate())

    def spread(self, buf, k, src=None):
        g = self.g
        own = buf.at[k, g.pair, g.line]
        for d in range(1, g.line_size):
            self.start(k, d - 1, own if src is None else src, own, g.line_size - 1 - d, g.device(g.ahead(d), g.pair))
        self.to_mate(buf, k, 0, src)

    def forward(self, buf, k):
        g = self.g
        for d in range(1, g.line_size):
            self.arrived(k, d - 1, buf.at[k, g.pair, g.ahead(d)])
            self.to_mate(buf, k, d)

    def finish(self, buf, k):
        g = self.g
        for d in range(g.line_size):
            self.arrived(k, g.line_size - 1 + d, buf.at[k, 1 - g.pair, g.ahead(d)])


class Scatter(Comm):
    def exchange(self, part, from_mate, k):
        g = self.g
        for d in [*range(1, g.line_size), 0]:
            to = g.ahead(d)
            slot = g.line_size - 1 + d
            self.start(k, slot, part.at[k, 1 - g.pair, to], from_mate.at[k, to], slot, g.mate())

    def pass_on(self, part, from_mate, from_line, k):
        g = self.g
        for d in range(1, g.line_size):
            to = g.ahead(d)
            self.arrived(k, g.line_size - 1 + d, from_mate.at[k, to])
            mine = part.at[k, g.pair, to]
            mine[...] = (mine[...].astype(F32) + from_mate[k, to].astype(F32)).astype(BF)
            slot = g.line_size - 1 - d
            self.start(k, d - 1, mine, from_line.at[k, slot], slot, g.device(to, g.pair))

    def landed(self, from_mate, from_line, k):
        g = self.g
        self.arrived(k, g.line_size - 1, from_mate.at[k, g.line])
        for e in range(g.line_size - 1):
            self.arrived(k, e, from_line.at[k, e])

    def total(self, part, from_mate, from_line, k, cols=slice(None)):
        g = self.g
        acc = part[k, g.pair, g.line, :, cols].astype(F32) + from_mate[k, g.line, :, cols].astype(F32)
        for e in range(g.line_size - 1):
            acc = acc + from_line[k, e, :, cols].astype(F32)
        return acc


def flat(value):
    return value.reshape(-1, value.shape[-1])


def turns(chunks, stages):
    if chunks == 4 and stages == 16:
        line = [int(c) for c in "".join(TURNS)]
    else:
        line = [k for _, _, k in sorted((s + k, -s, k) for k in range(chunks) for s in range(stages))]
    for _ in range(line.count(chunks - 1) - (stages - 2)):
        line.pop(len(line) - 1 - line[::-1].index(chunks - 1))
    done = [0] * chunks
    order = []
    for k in line:
        order.append((k, done[k]))
        done[k] += 1
    return order


def tile_of(size):
    return next(t for t in (512, 256, 128) if size % t == 0)


def last_last(left, right):
    return lax.dot_general(left, right, (((1,), (1,)), ((), ())), preferred_element_type=F32)


def layer_kernel(
    rows_n, cols_n,
    x_ref, target_hbm, wg_hbm, wu_hbm, wd_hbm,
    out_ref, gx_ref, tok_hbm, hid_hbm, err_hbm, grad_hbm, part_hbm,
    wg, wu, wd, target, tok, hid, err, grad,
    p1, m1, l1, p2, m2, l2, p3, m3, l3, p4, m4, l4,
    row_send, row_recv, col_send, col_recv, load_sem, store_sem,
):
    hidden = wg.shape[1]
    feats = wg.shape[0]
    chunks = tok.shape[0]
    tb = tok.shape[3]
    row = Group("row", rows_n, "col")
    col = Group("col", cols_n, "row")

    loads = [
        pltpu.make_async_copy(wg_hbm, wg, load_sem.at[0]),
        pltpu.make_async_copy(wu_hbm, wu, load_sem.at[1]),
        pltpu.make_async_copy(wd_hbm, wd, load_sem.at[2]),
        pltpu.make_async_copy(
            target_hbm.at[pl.ds(pl.multiple_of(lax.axis_index("col") * tb * chunks, tb * chunks), tb * chunks)],
            target, load_sem.at[3],
        ),
    ]

    barrier = pltpu.get_barrier_semaphore()
    peers = []
    for g in (row, col):
        peers.append(g.mate())
        for d in range(1, g.line_size):
            peers.append(g.device(g.ahead(d), g.pair))
    for peer in peers:
        pl.semaphore_signal(barrier, inc=1, device_id=peer, device_id_type=MESH)
    pl.semaphore_wait(barrier, len(peers))

    sent, stores = [], []
    ag_in = Gather(col, col_send.at[0], col_recv.at[0], sent)
    rs_act = Scatter(row, row_send.at[0], row_recv.at[0], sent)
    ag_hid = Gather(row, row_send.at[1], row_recv.at[1], sent)
    rs_out = Scatter(col, col_send.at[1], col_recv.at[1], sent)
    ag_err = Gather(col, col_send.at[2], col_recv.at[2], sent)
    rs_hid = Scatter(row, row_send.at[2], row_recv.at[2], sent)
    ag_grad = Gather(row, row_send.at[3], row_recv.at[3], sent)
    rs_in = Scatter(col, col_send.at[3], col_recv.at[3], sent)

    def store(buf, out, i, k):
        copy = pltpu.make_async_copy(buf.at[k], out.at[k], store_sem.at[i, k])
        copy.start()
        stores.append(copy)

    waited = set()

    def need(i):
        if i not in waited:
            waited.add(i)
            loads[i].wait()

    def tiles(size, body):
        t = tile_of(size)

        def step(j, _):
            body(pl.ds(pl.multiple_of(j * t, t), t), j * t)
            return 0

        lax.fori_loop(0, size // t, step, 0)

    def put(part, k, cols, value):
        shape = part.shape[1:4] + (value.shape[-1],)
        part[k, :, :, :, cols] = value.astype(BF).reshape(shape)

    def token_rows(k):
        return pl.ds(k * tb, tb)

    def s_in(k):
        tok[k, col.pair, col.line] = x_ref[token_rows(k), :]
        ag_in.spread(tok, k, x_ref.at[token_rows(k)])

    def s_in_fwd(k):
        ag_in.forward(tok, k)

    def s_act(k):
        ag_in.finish(tok, k)
        need(0)
        need(1)

        def body(cols, at):
            t = cols.size
            put(p1, k, cols, jnp.dot(flat(tok[k]), wg[:, cols], preferred_element_type=F32))
            ups = pl.ds(pl.multiple_of(hidden + at, t), t)
            put(p1, k, ups, jnp.dot(flat(tok[k]), wu[:, cols], preferred_element_type=F32))

        tiles(hidden, body)
        rs_act.exchange(p1, m1, k)
        store(tok, tok_hbm, 0, k)

    def s_act_pass(k):
        rs_act.pass_on(p1, m1, l1, k)

    def s_hid(k):
        rs_act.landed(m1, l1, k)
        gate = rs_act.total(p1, m1, l1, k, pl.ds(0, hidden))
        up = rs_act.total(p1, m1, l1, k, pl.ds(hidden, hidden))
        hid[k, row.pair, row.line] = (gate * jax.nn.sigmoid(gate) * up).astype(BF)
        ag_hid.spread(hid, k)

    def s_hid_fwd(k):
        ag_hid.forward(hid, k)

    def s_out(k):
        ag_hid.finish(hid, k)
        need(2)
        tiles(feats, lambda cols, at: put(
            p2, k, cols, jnp.dot(flat(hid[k]), wd[:, cols], preferred_element_type=F32)))
        rs_out.exchange(p2, m2, k)
        store(hid, hid_hbm, 1, k)

    def s_out_pass(k):
        rs_out.pass_on(p2, m2, l2, k)

    def s_err(k):
        rs_out.landed(m2, l2, k)
        need(3)
        result = rs_out.total(p2, m2, l2, k)
        out_ref[token_rows(k), :] = result.astype(BF)
        err[k, col.pair, col.line] = (result - target[token_rows(k), :].astype(F32)).astype(BF)
        ag_err.spread(err, k)

    def s_err_fwd(k):
        ag_err.forward(err, k)

    def s_ghid(k):
        ag_err.finish(err, k)
        tiles(hidden, lambda cols, at: put(p3, k, cols, last_last(flat(err[k]), wd[cols, :])))
        rs_hid.exchange(p3, m3, k)
        store(err, err_hbm, 2, k)

    def s_ghid_pass(k):
        rs_hid.pass_on(p3, m3, l3, k)

    def s_grads(k):
        rs_hid.landed(m3, l3, k)
        gate = rs_act.total(p1, m1, l1, k, pl.ds(0, hidden))
        up = rs_act.total(p1, m1, l1, k, pl.ds(hidden, hidden))
        dh = rs_hid.total(p3, m3, l3, k)
        sigma = jax.nn.sigmoid(gate)
        grad[k, row.pair, row.line, :, pl.ds(0, hidden)] = (
            dh * up * sigma * (1.0 + gate * (1.0 - sigma))).astype(BF)
        grad[k, row.pair, row.line, :, pl.ds(hidden, hidden)] = (dh * (gate * sigma)).astype(BF)
        ag_grad.spread(grad, k)

    def s_grads_fwd(k):
        ag_grad.forward(grad, k)

    def s_gin(k):
        ag_grad.finish(grad, k)
        tiles(feats, lambda cols, at: put(
            p4, k, cols,
            last_last(flat(grad[k, :, :, :, pl.ds(0, hidden)]), wg[cols, :])
            + last_last(flat(grad[k, :, :, :, pl.ds(hidden, hidden)]), wu[cols, :])))
        store(grad, grad_hbm, 3, k)
        if k < chunks - 1:
            rs_in.exchange(p4, m4, k)
            return
        copy = pltpu.make_async_copy(p4.at[k], part_hbm, load_sem.at[4])
        copy.start()
        stores.append(copy)

    def s_gin_pass(k):
        rs_in.pass_on(p4, m4, l4, k)

    def s_gout(k):
        rs_in.landed(m4, l4, k)
        gx_ref[token_rows(k), :] = rs_in.total(p4, m4, l4, k).astype(BF)

    stages = [
        s_in_fwd, s_act, s_act_pass, s_hid, s_hid_fwd, s_out, s_out_pass, s_err, s_err_fwd,
        s_ghid, s_ghid_pass, s_grads, s_grads_fwd, s_gin, s_gin_pass, s_gout,
    ]
    for k in range(chunks):
        s_in(k)
    for copy in loads:
        copy.start()
    for k, s in turns(chunks, len(stages)):
        stages[s](k)
    for copy in sent:
        copy.wait_send()
    for copy in stores:
        copy.wait()


def run_layer(rows_n, cols_n, inputs, target, gate_weight, up_weight, down_weight):
    own, feats = inputs.shape
    hidden = gate_weight.shape[1]
    chunks = CHUNKS
    while chunks > 1 and (own % (16 * chunks) or (own * cols_n) % (16 * chunks * rows_n)):
        chunks //= 2
    tb = own // chunks
    rb = own * cols_n // chunks // rows_n
    rl, cl = rows_n // 2, cols_n // 2

    def by_col(width):
        return (chunks, 2, cl, tb, width)

    def by_row(width):
        return (chunks, 2, rl, rb, width)

    def scatter_bufs(line, rows, width):
        return [
            pltpu.VMEM((chunks, 2, line, rows, width), BF),
            pltpu.VMEM((chunks, line, rows, width), BF),
            pltpu.VMEM((chunks, line - 1, rows, width), BF),
        ]

    anywhere = pl.BlockSpec(memory_space=pl.ANY)
    vmem = pl.BlockSpec(memory_space=pltpu.VMEM)
    kept = [by_col(feats), by_row(hidden), by_col(feats), by_row(2 * hidden)]
    return pl.pallas_call(
        functools.partial(layer_kernel, rows_n, cols_n),
        out_shape=[
            jax.ShapeDtypeStruct(s, BF)
            for s in [(own, feats), (max(own - tb, tb), feats), *kept, by_col(feats)[1:]]
        ],
        in_specs=[vmem] + [anywhere] * 4,
        out_specs=[vmem] * 2 + [anywhere] * 5,
        scratch_shapes=[
            pltpu.VMEM(gate_weight.shape, BF),
            pltpu.VMEM(up_weight.shape, BF),
            pltpu.VMEM(down_weight.shape, BF),
            pltpu.VMEM((own, feats), BF),
            *[pltpu.VMEM(s, BF) for s in kept],
            *scatter_bufs(rl, rb, 2 * hidden),
            *scatter_bufs(cl, tb, feats),
            *scatter_bufs(rl, rb, hidden),
            *scatter_bufs(cl, tb, feats),
            pltpu.SemaphoreType.DMA((4, chunks, 2 * rl - 1)),
            pltpu.SemaphoreType.DMA((4, chunks, 2 * rl - 1)),
            pltpu.SemaphoreType.DMA((4, chunks, 2 * cl - 1)),
            pltpu.SemaphoreType.DMA((4, chunks, 2 * cl - 1)),
            pltpu.SemaphoreType.DMA((5,)),
            pltpu.SemaphoreType.DMA((4, chunks)),
        ],
        compiler_params=pltpu.CompilerParams(
            collective_id=0, has_side_effects=True, vmem_limit_bytes=60 * 2**20
        ),
        cost_estimate=pl.CostEstimate(
            flops=12 * own * cols_n * feats * hidden,
            bytes_accessed=6 * feats * hidden,
            transcendentals=0,
        ),
        name="layer",
    )(inputs, target, gate_weight, up_weight, down_weight)


def finish_scatter(part, cols_n):
    me = lax.axis_index("col")

    def block(c):
        return part[lax.rem(c, 2), lax.div(c, 2)]

    total = block(me).astype(F32)
    for d in range(1, cols_n):
        pairs = [(c, (c + d) % cols_n) for c in range(cols_n)]
        total = total + lax.ppermute(block(lax.rem(me + d, cols_n)), "col", pairs).astype(F32)
    return total.astype(BF)


def outer_kernel(n, left_ref, *refs):
    turned = left_ref[...].T
    for right_ref, out_ref in zip(refs[:n], refs[n:]):
        out_ref[...] = jnp.dot(turned, right_ref[...], preferred_element_type=F32).astype(BF)


def outer_products(left, rights):
    tokens, wide = left.shape
    step = next(t for t in (512, 256, 128) if wide % t == 0)
    width = rights[0][2]
    return pl.pallas_call(
        functools.partial(outer_kernel, len(rights)),
        grid=(wide // step,),
        out_shape=[jax.ShapeDtypeStruct((wide, width), BF)] * len(rights),
        in_specs=[pl.BlockSpec((tokens, step), lambda i: (0, i))]
        + [pl.BlockSpec((tokens, width), functools.partial(lambda at, i: (0, at), at)) for _, at, _ in rights],
        out_specs=[pl.BlockSpec((step, width), lambda i: (i, 0))] * len(rights),
        compiler_params=pltpu.CompilerParams(vmem_limit_bytes=60 * 2**20),
        cost_estimate=pl.CostEstimate(
            flops=2 * tokens * wide * width * len(rights),
            bytes_accessed=2 * (tokens * wide + (tokens + wide) * width * len(rights)),
            transcendentals=0,
        ),
        name="outer",
    )(left, *[r for r, _, _ in rights])


def body(rows_n, cols_n, inputs, target, gate_weight, up_weight, down_weight):
    output, first_rows, tok, hid, err, grad, part = run_layer(
        rows_n, cols_n, inputs, target, gate_weight, up_weight, down_weight)
    last_rows = finish_scatter(part, cols_n)
    kept_rows = inputs.shape[0] - last_rows.shape[0]
    grad_inputs = jnp.concatenate([first_rows[:kept_rows], last_rows], axis=0)
    tok, hid, err, grad = (flat(a) for a in (tok, hid, err, grad))
    hidden = gate_weight.shape[1]
    grad_gate_weight, grad_up_weight = outer_products(tok, [(grad, 0, hidden), (grad, 1, hidden)])
    (grad_down_weight,) = outer_products(hid, [(err, 0, err.shape[1])])
    return (output, grad_inputs, grad_gate_weight, grad_up_weight, grad_down_weight)


def solution(mesh):
    placed = (P("col", "row"), P(None, "row"), P("row", "col"), P("row", "col"), P("col", "row"))
    return jax.shard_map(
        functools.partial(body, mesh.shape["row"], mesh.shape["col"]),
        mesh=mesh,
        in_specs=placed,
        out_specs=(
            P("col", "row"),
            P("col", "row"),
            P("row", "col"),
            P("row", "col"),
            P("col", "row"),
        ),
        check_vma=False,
    )
```
